32 devices in a mesh: groups: 2 (over y), col: 4 (over z), row: 4 (over x, core).
Axes of the slice: x: 2, y: 2, z: 4, core: 2. Of those that a mesh axis runs over, the one named last changes fastest.
Arguments:
- x_stored: bfloat16 [1024, 9216], P(('groups', 'row'), 'col'), parts along dimension 0, may hold values from -6 to 6
- group_units: int32 [64], replicated, may hold values from 1 to 12, 288 in all
- group_order: int32 [64], replicated, may hold values from 0 to 63, each once
- up_weight: bfloat16 [9216, 36864], P('row', 'col'), may hold values from -0.0625 to 0.0625
- down_weight: bfloat16 [36864, 9216], P('col', 'row'), may hold values from -0.03125 to 0.03125
Outputs:
- mixed: bfloat16 [1024, 9216], P(('groups', 'col'), 'row'), parts along dimension 0
The draws below stay inside these ranges and needn't reach their ends.
There are 2 independent parts, one for each index of `groups`. The reference program is written for one: setup_inputs(seed, part) draws one part's arguments, and reference() takes and returns one part's arrays. A program takes and returns all parts, laid end to end along the dimension named above; an argument that names none is the same for every part. Nothing has to cross between parts.
Inputs may be any that keep to these rules, and one draw needn't show every extreme that they name: `group_units`: sizes in blocks of 32 features; they sum to 288, and one group has exactly 12. `group_order`: each group number appears once.
All inputs are finite; a program needn't handle non-finite values.
Results may differ from the reference program's by a relative error of at most 0.0095.
Values may be sent and summed in bfloat16 or wider, within the bound.
A program may use at most 256 MiB of HBM per device.

```python
import math
import jax
import jax.numpy as jnp
import numpy as np
from jax import lax

D = 9216
FF = 36864
BLOCK = 32
GROUPS = 64
MOST = 12
TOKENS = 512
UNITS = 288
N_COL = 4


def block_scale(stream_key, extent, pieces, low, top_value):
    level, own = 1.0, jax.random.fold_in(stream_key, 6)
    for axis_at, parts in pieces:
        heights = jnp.exp(jax.random.uniform(jax.random.fold_in(own, axis_at), (parts,), jnp.float32, low / len(pieces), top_value / len(pieces)))
        level = level * jnp.repeat(heights, extent[axis_at] // parts).reshape([-1 if axis == axis_at else 1 for axis in range(len(extent))])
    return level


def profile(count, total, bound, slope):
    weights = [(1 << 20) // math.isqrt(standing ** slope) + 1 for standing in range(2, count + 1)]
    spare, holding = total - bound - (count - 1), [1] * (count - 1)
    while spare > 0:
        candidates = [i for i in range(count - 1) if holding[i] < bound]
        whole, budget = sum([weights[i] for i in candidates]), spare
        for i in candidates:
            more = min(bound - holding[i], max(1, budget * weights[i] // whole), spare)
            holding[i] = holding[i] + more
            spare = spare - more
    return np.array([bound] + holding)


def uneven(own_key, number_of, total, bound, skew):
    if number_of == 2:
        one = jax.random.randint(own_key, (), max(1, total - bound), min(bound, total - 1) + 1)
        return jnp.stack([one, total - one])
    tallies = jnp.asarray(profile(number_of, total, bound, skew), jnp.int32)
    pairs = (number_of - 1) // 2
    source_of, taker = tallies[1:1 + 2 * pairs:2], tallies[2:2 + 2 * pairs:2]
    slack = jnp.minimum(source_of - 1, bound - taker)
    shifted = jax.random.randint(jax.random.fold_in(own_key, 1), (pairs,), 0, 1 << 20) % (slack + 1)
    tallies = tallies.at[1:1 + 2 * pairs:2].set(source_of - shifted).at[2:2 + 2 * pairs:2].set(taker + shifted)
    return tallies[jax.random.permutation(jax.random.fold_in(own_key, 2), number_of)]


def normal_values(stream_key, shape, deviation, bound, split=(), held_as=jnp.bfloat16):
    array = jax.random.normal(stream_key, shape, jnp.float32) * deviation
    if len(split) > 0:
        array = block_scale(stream_key, shape, split, -0.22, 0.18) * array
    return jnp.clip(array, min=-bound, max=bound).astype(held_as)


def setup_inputs(seed: int = 0, part: int = 0) -> dict:
    key_of = jax.random.split(jax.random.key(seed), 6)
    own_keys = jax.random.split(jax.random.fold_in(key_of[5], part), 6)
    x_stored = normal_values(own_keys[0], (TOKENS, D), 1.0, 6.0, ((0, 4), (1, 4)))
    group_units = uneven(key_of[1], GROUPS, UNITS, MOST, 2).astype(jnp.int32)
    group_order = jax.random.permutation(key_of[2], GROUPS).astype(jnp.int32)
    up_weight = normal_values(key_of[3], (D, FF), D ** -0.5, 0.0625, ((0, 4), (1, 4)))
    down_weight = normal_values(key_of[4], (FF, D), FF ** -0.5, 0.03125, ((0, 4), (1, 4)))
    return dict(x_stored=x_stored, group_units=group_units, group_order=group_order, up_weight=up_weight, down_weight=down_weight)


def unit_source(group_units, group_order):
    count = group_units.shape[0]
    group_ids = jnp.arange(count, dtype=jnp.int32)
    onehot = (group_order[:, None] == group_ids[None, :]).astype(jnp.int32)
    canon_start = (jnp.cumsum(group_units) - group_units).astype(jnp.int32)
    slot_length = jnp.sum(onehot * group_units[None, :], axis=1).astype(jnp.int32)
    slot_canon = jnp.sum(onehot * canon_start[None, :], axis=1).astype(jnp.int32)
    slot_start = (jnp.cumsum(slot_length) - slot_length).astype(jnp.int32)
    unit_ids = jnp.arange(UNITS, dtype=jnp.int32)
    inside = (unit_ids[:, None] >= slot_start[None, :]) & (unit_ids[:, None] < (slot_start + slot_length)[None, :])
    canon_unit = jnp.sum(jnp.where(inside, slot_canon[None, :] + unit_ids[:, None] - slot_start[None, :], 0), axis=1).astype(jnp.int32)
    source = jnp.sum(jnp.where(canon_unit[None, :] == unit_ids[:, None], unit_ids[None, :], 0), axis=1)
    return source.astype(jnp.int32)


def column_list(source):
    offsets = jnp.arange(BLOCK, dtype=jnp.int32)
    return (source[:, None] * BLOCK + offsets[None, :]).reshape(-1).astype(jnp.int32)


def exponent_floor(magnitude, lowest, highest, offset):
    result = jnp.full(magnitude.shape, 2.0 ** (lowest + offset), jnp.float32)
    for power in range(lowest + 1, highest + 1):
        result = jnp.where(magnitude >= 2.0 ** power, jnp.float32(2.0 ** (power + offset)), result)
    return result


def encode(values):
    row_total = values.shape[0]
    blocks = values.astype(jnp.float32).reshape(row_total, -1, BLOCK)
    largest = jnp.max(jnp.abs(blocks), axis=2)
    scale = exponent_floor(largest, -20, 8, -8)
    magnitude = jnp.abs(blocks) / scale[:, :, None]
    spacing = exponent_floor(magnitude, -6, 8, -3)
    level = jnp.minimum(jnp.floor(magnitude / spacing + 0.5) * spacing, 448.0)
    encoded = jnp.where(blocks < 0.0, -level, level).astype(jnp.bfloat16)
    return encoded.reshape(row_total, -1), scale.astype(jnp.bfloat16)


def decode(encoded, scales):
    row_total = encoded.shape[0]
    blocks = encoded.astype(jnp.float32).reshape(row_total, -1, BLOCK) * scales.astype(jnp.float32)[:, :, None]
    return blocks.astype(jnp.bfloat16).reshape(row_total, -1)


def reference(x_stored, group_units, group_order, up_weight, down_weight):
    source = unit_source(group_units, group_order)
    x_canon = jnp.take(x_stored, column_list(source), axis=1)
    encoded, scales = encode(x_canon)
    panels = decode(encoded, scales)
    summed = jnp.dot(panels, up_weight, preferred_element_type=jnp.float32)
    hidden = jnp.square(jnp.maximum(summed, 0.0)).astype(jnp.bfloat16)
    shard = FF // N_COL

    def add_part(shard_index, running):
        left = lax.dynamic_slice_in_dim(hidden, shard_index * shard, shard, 1)
        right = lax.dynamic_slice_in_dim(down_weight, shard_index * shard, shard, 0)
        partial_value = jnp.dot(left, right, preferred_element_type=jnp.float32)
        return running + partial_value.astype(jnp.bfloat16).astype(jnp.float32)

    mixed = lax.fori_loop(0, N_COL, add_part, jnp.zeros((TOKENS, D), jnp.float32))
    return mixed.astype(jnp.bfloat16)
```

```python
import functools
import jax
import jax.numpy as jnp
from jax import lax
from jax.experimental import pallas as pl
from jax.experimental.pallas import tpu as pltpu
from jax.sharding import PartitionSpec as P

BLOCK = 32
UNITS = 288
MESH = pl.DeviceIdType.MESH
LAG = 5


def unit_source(group_units, group_order):
    count = group_units.shape[0]
    group_ids = jnp.arange(count, dtype=jnp.int32)
    onehot = (group_order[:, None] == group_ids[None, :]).astype(jnp.int32)
    canon_start = jnp.cumsum(group_units) - group_units
    slot_length = jnp.sum(onehot * group_units[None, :], axis=1)
    slot_canon = jnp.sum(onehot * canon_start[None, :], axis=1)
    slot_start = jnp.cumsum(slot_length) - slot_length
    unit_ids = jnp.arange(UNITS, dtype=jnp.int32)
    inside = (unit_ids[:, None] >= slot_start[None, :]) & (
        unit_ids[:, None] < (slot_start + slot_length)[None, :]
    )
    canon_unit = jnp.sum(
        jnp.where(inside, slot_canon[None, :] + unit_ids[:, None] - slot_start[None, :], 0), axis=1
    )
    source = jnp.sum(
        jnp.where(canon_unit[None, :] == unit_ids[:, None], unit_ids[None, :], 0), axis=1
    )
    return source


def exponent_floor(magnitude, lowest, highest, offset):
    result = jnp.full(magnitude.shape, 2.0 ** (lowest + offset), jnp.float32)
    for power in range(lowest + 1, highest + 1):
        result = jnp.where(magnitude >= 2.0**power, jnp.float32(2.0 ** (power + offset)), result)
    return result


def block_scaled(values):
    features, tokens = values.shape
    blocks = values.astype(jnp.float32).reshape(features // BLOCK, BLOCK, tokens)
    largest = jnp.max(jnp.abs(blocks), axis=1)
    scale = exponent_floor(largest, -20, 8, -8)[:, None, :]
    magnitude = jnp.abs(blocks) / scale
    spacing = exponent_floor(magnitude, -6, 8, -3)
    level = jnp.minimum(jnp.floor(magnitude / spacing + 0.5) * spacing, 448.0)
    panels = jnp.where(blocks < 0.0, -level, level) * scale
    return panels.astype(jnp.bfloat16)


def middle_kernel(passes, chunks, width, panel_ref, up_ref, down_ref, out_ref,
                  near, hand, far, hid, total, up_buf, down_buf,
                  up_sem, down_sem, near_send, near_recv, far_send, far_recv, hid_send, hid_recv):
    items = passes * chunks
    half = near.shape[1]
    row = lax.axis_index("row")
    sibling = row + 1 - 2 * lax.rem(row, 2)
    partner = lax.rem(row + 2, 4)

    barrier = pltpu.get_barrier_semaphore()
    for other in (sibling, partner):
        pl.semaphore_signal(barrier, inc=1, device_id={"row": other}, device_id_type=MESH)

    def up_copy(item):
        slot = lax.rem(item, 2)
        columns = pl.ds(pl.multiple_of(lax.rem(item, chunks) * width, width), width)
        return pltpu.make_async_copy(up_ref.at[:, columns], up_buf.at[slot], up_sem.at[slot])

    def down_copy(item):
        slot = lax.rem(item, 2)
        rows = pl.ds(pl.multiple_of(lax.rem(item, chunks) * width, width), width)
        return pltpu.make_async_copy(down_ref.at[rows, :], down_buf.at[slot], down_sem.at[slot])

    def to_near(item):
        return pltpu.make_async_remote_copy(
            src_ref=near.at[item], dst_ref=hand.at[item], send_sem=near_send.at[item],
            recv_sem=near_recv.at[item], device_id={"row": sibling}, device_id_type=MESH)

    def to_far(item):
        return pltpu.make_async_remote_copy(
            src_ref=far.at[item], dst_ref=hid.at[item, 0], send_sem=far_send.at[item],
            recv_sem=far_recv.at[item], device_id={"row": partner}, device_id_type=MESH)

    def to_hid(item):
        return pltpu.make_async_remote_copy(
            src_ref=hid.at[item, 0], dst_ref=hid.at[item, 1], send_sem=hid_send.at[item],
            recv_sem=hid_recv.at[item], device_id={"row": sibling}, device_id_type=MESH)

    up_copy(0).start()
    up_copy(1).start()
    down_copy(0).start()
    down_copy(1).start()
    pl.semaphore_wait(barrier, 2)

    def step(t, carry):
        @pl.when(t < items)
        def _():
            up_copy(t).wait()
            slot = lax.rem(t, 2)
            product = jnp.dot(panel_ref[lax.div(t, chunks)], up_buf[slot],
                              preferred_element_type=jnp.float32)
            near[t] = product[half:].astype(jnp.bfloat16)
            to_near(t).start()
            far[t] = product[:half].astype(jnp.bfloat16)

            @pl.when(t + 2 < items)
            def _():
                up_copy(t + 2).start()

        @pl.when((t >= 1) & (t < items + 1))
        def _():
            item = t - 1
            to_near(item).wait_recv()
            far[item] = (far[item].astype(jnp.float32) + hand[item].astype(jnp.float32)).astype(jnp.bfloat16)
            to_far(item).start()

        @pl.when((t >= LAG) & (t < items + LAG))
        def _():
            item = t - LAG
            to_far(item).wait_recv()
            summed = far[item].astype(jnp.float32) + hid[item, 0].astype(jnp.float32)
            hid[item, 0] = jnp.square(jnp.maximum(summed, 0.0)).astype(jnp.bfloat16)
            to_hid(item).start()

        @pl.when(t >= LAG + 1)
        def _():
            item = t - LAG - 1
            slot = lax.rem(item, 2)
            place = lax.rem(item, chunks)
            to_hid(item).wait_recv()
            down_copy(item).wait()
            product = jnp.dot(hid[item].reshape(2 * half, width), down_buf[slot],
                              preferred_element_type=jnp.float32)

            @pl.when(place == 0)
            def _():
                total[...] = product

            @pl.when(place > 0)
            def _():
                total[...] += product

            @pl.when(item + 2 < items)
            def _():
                down_copy(item + 2).start()

            @pl.when(place == chunks - 1)
            def _():
                out_ref[lax.div(item, chunks)] = total[...].astype(jnp.bfloat16)

        return carry

    lax.fori_loop(0, items + LAG + 1, step, 0)

    def drain(item, carry):
        to_near(item).wait_send()
        to_far(item).wait_send()
        to_hid(item).wait_send()
        return carry

    lax.fori_loop(0, items, drain, 0)


def middle(panels, up_weight, down_weight):
    passes, tokens, depth = panels.shape
    hidden = up_weight.shape[1]
    columns = down_weight.shape[1]
    width = next(w for w in (512, 384, 256, 128) if hidden % w == 0)
    chunks = hidden // width
    items = passes * chunks
    half = tokens // 2
    flops = 2 * passes * tokens * hidden * (depth + columns)
    return pl.pallas_call(
        functools.partial(middle_kernel, passes, chunks, width),
        out_shape=jax.ShapeDtypeStruct((passes, tokens, columns), jnp.bfloat16),
        in_specs=[pl.BlockSpec(memory_space=pltpu.VMEM), pl.BlockSpec(memory_space=pl.ANY),
                  pl.BlockSpec(memory_space=pl.ANY)],
        out_specs=pl.BlockSpec(memory_space=pltpu.VMEM),
        scratch_shapes=[
            pltpu.VMEM((items, half, width), jnp.bfloat16),
            pltpu.VMEM((items, half, width), jnp.bfloat16),
            pltpu.VMEM((items, half, width), jnp.bfloat16),
            pltpu.VMEM((items, 2, half, width), jnp.bfloat16),
            pltpu.VMEM((tokens, columns), jnp.float32),
            pltpu.VMEM((2, depth, width), jnp.bfloat16),
            pltpu.VMEM((2, width, columns), jnp.bfloat16),
            pltpu.SemaphoreType.DMA((2,)),
            pltpu.SemaphoreType.DMA((2,)),
        ] + [pltpu.SemaphoreType.DMA((items,))] * 6,
        compiler_params=pltpu.CompilerParams(
            collective_id=0, has_side_effects=True, vmem_limit_bytes=58 * 1024 * 1024),
        cost_estimate=pl.CostEstimate(flops=flops, transcendentals=0,
                                      bytes_accessed=2 * passes * (up_weight.size + down_weight.size)),
    )(panels, up_weight, down_weight)


def on_device(x_stored, group_units, group_order, up_weight, down_weight):
    rows, cols = lax.axis_size("row"), lax.axis_size("col")
    share = x_stored.shape[0]
    tokens = rows * share
    part = tokens // cols
    passes = 2 if part % 32 == 0 else 1
    source = unit_source(group_units, group_order)
    panels = block_scaled(x_stored.T)
    panels = lax.all_gather(panels, "col", axis=0, tiled=True)
    panels = jnp.take(panels.reshape(UNITS, BLOCK, share), source, axis=0)
    panels = lax.all_to_all(panels.reshape(rows, -1, share), "row", split_axis=0, concat_axis=0, tiled=True)
    panels = panels.transpose(0, 2, 1)
    depth = panels.shape[2]
    core = lax.rem(lax.axis_index("row"), 2)
    panels = panels.reshape(rows // 2, 2, passes, share // passes, depth)
    panels = panels.transpose(2, 1, 0, 3, 4)
    panels = jnp.where(core == 0, panels, panels[:, ::-1])
    partial = middle(panels.reshape(passes, tokens // passes, depth), up_weight, down_weight)
    partial = partial.reshape(passes, 2, rows // 2, share // passes, -1)
    partial = jnp.where(core == 0, partial, partial[:, ::-1])
    partial = partial.transpose(2, 1, 0, 3, 4).reshape(tokens, -1)
    return lax.psum_scatter(partial, "col", scatter_dimension=0, tiled=True)


def solution(mesh):
    in_specs = (P(("groups", "row"), "col"), P(), P(), P("row", "col"), P("col", "row"))
    out_specs = P(("groups", "col"), "row")
    return jax.shard_map(
        on_device, mesh=mesh, in_specs=in_specs, out_specs=out_specs, check_vma=False
    )
```

```python
import functools
import jax
import jax.numpy as jnp
from jax import lax
from jax.experimental import pallas as pl
from jax.experimental.pallas import tpu as pltpu
from jax.sharding import PartitionSpec as P

BLOCK = 32
UNITS = 288
MESH = pl.DeviceIdType.MESH
LAG = 5
NEAR = 4


def unit_source(group_units, group_order):
    count = group_units.shape[0]
    group_ids = jnp.arange(count, dtype=jnp.int32)
    onehot = (group_order[:, None] == group_ids[None, :]).astype(jnp.int32)
    canon_start = jnp.cumsum(group_units) - group_units
    slot_length = jnp.sum(onehot * group_units[None, :], axis=1)
    slot_canon = jnp.sum(onehot * canon_start[None, :], axis=1)
    slot_start = jnp.cumsum(slot_length) - slot_length
    unit_ids = jnp.arange(UNITS, dtype=jnp.int32)
    inside = (unit_ids[:, None] >= slot_start[None, :]) & (
        unit_ids[:, None] < (slot_start + slot_length)[None, :]
    )
    canon_unit = jnp.sum(
        jnp.where(inside, slot_canon[None, :] + unit_ids[:, None] - slot_start[None, :], 0), axis=1
    )
    source = jnp.sum(
        jnp.where(canon_unit[None, :] == unit_ids[:, None], unit_ids[None, :], 0), axis=1
    )
    return source


def exponent_floor(magnitude, lowest, highest, offset):
    result = jnp.full(magnitude.shape, 2.0 ** (lowest + offset), jnp.float32)
    for power in range(lowest + 1, highest + 1):
        result = jnp.where(magnitude >= 2.0**power, jnp.float32(2.0 ** (power + offset)), result)
    return result


def block_scaled(values):
    features, tokens = values.shape
    blocks = values.astype(jnp.float32).reshape(features // BLOCK, BLOCK, tokens)
    largest = jnp.max(jnp.abs(blocks), axis=1)
    scale = exponent_floor(largest, -20, 8, -8)[:, None, :]
    magnitude = jnp.abs(blocks) / scale
    spacing = exponent_floor(magnitude, -6, 8, -3)
    level = jnp.minimum(jnp.floor(magnitude / spacing + 0.5) * spacing, 448.0)
    panels = jnp.where(blocks < 0.0, -level, level) * scale
    return panels.astype(jnp.bfloat16)


def layer_kernel(passes, chunks, width, *refs):
    place_ref, lane_ref, x_ref, up_ref, down_ref, out_ref = refs[:6]
    gather = refs[6:6 + passes]
    (moved, blocks, panel, near, mine, hand, far, hid, total, own, parts, up_buf, down_buf,
     keep_sem, gather_send, gather_recv, moved_send, moved_recv, up_sem, down_sem, near_send, near_recv,
     far_send, far_recv, hid_send, hid_recv, part_send, part_recv) = refs[6 + passes:]
    items = passes * chunks
    half = hand.shape[1]
    cols, seg = own.shape[1], own.shape[2]
    units, lanes = blocks.shape[2], blocks.shape[4]
    local = x_ref.shape[1]
    piece = lanes // passes
    columns = out_ref.shape[1]
    row, col = lax.axis_index("row"), lax.axis_index("col")
    core = lax.rem(row, 2)
    sibling = row + 1 - 2 * core
    partner = lax.rem(row + 2, 4)
    across = lax.rem(sibling + 2, 4)

    barrier = pltpu.get_barrier_semaphore()
    for other in (sibling, partner, across):
        pl.semaphore_signal(barrier, inc=1, device_id={"row": other}, device_id_type=MESH)
    for k in range(1, cols):
        pl.semaphore_signal(barrier, inc=1, device_id={"col": lax.rem(col + k, cols)}, device_id_type=MESH)

    def keep(p):
        return pltpu.make_async_copy(x_ref.at[p], gather[p].at[pl.ds(col * local, local)], keep_sem.at[p])

    def to_col(p, k):
        return pltpu.make_async_remote_copy(
            src_ref=x_ref.at[p], dst_ref=gather[p].at[pl.ds(col * local, local)], send_sem=gather_send.at[p, k],
            recv_sem=gather_recv.at[p, k], device_id={"col": lax.rem(col + k, cols)}, device_id_type=MESH)

    def to_row(p, k):
        target = (row, partner, across, sibling)[k]
        return pltpu.make_async_remote_copy(
            src_ref=moved.at[p, k - 1], dst_ref=blocks.at[p, k], send_sem=moved_send.at[p, k - 1],
            recv_sem=moved_recv.at[p, k - 1], device_id={"row": target}, device_id_type=MESH)

    def up_copy(item):
        slot = lax.rem(item, 2)
        chunk = pl.ds(pl.multiple_of(lax.rem(item, chunks) * width, width), width)
        return pltpu.make_async_copy(up_ref.at[:, chunk], up_buf.at[slot], up_sem.at[slot])

    def down_copy(item):
        slot = lax.rem(item, 2)
        chunk = pl.ds(pl.multiple_of(lax.rem(item, chunks) * width, width), width)
        return pltpu.make_async_copy(down_ref.at[chunk, :], down_buf.at[slot], down_sem.at[slot])

    def to_near(item):
        slot = lax.rem(item, NEAR)
        return pltpu.make_async_remote_copy(
            src_ref=near.at[slot], dst_ref=hand.at[item], send_sem=near_send.at[slot],
            recv_sem=near_recv.at[item], device_id={"row": sibling}, device_id_type=MESH)

    def to_far(item):
        return pltpu.make_async_remote_copy(
            src_ref=far.at[item], dst_ref=hid.at[item, 0], send_sem=far_send.at[item],
            recv_sem=far_recv.at[item], device_id={"row": partner}, device_id_type=MESH)

    def to_hid(item):
        return pltpu.make_async_remote_copy(
            src_ref=hid.at[item, 0], dst_ref=hid.at[item, 1], send_sem=hid_send.at[item],
            recv_sem=hid_recv.at[item], device_id={"row": sibling}, device_id_type=MESH)

    def to_part(p, k):
        return pltpu.make_async_remote_copy(
            src_ref=own.at[p, k], dst_ref=parts.at[p, k], send_sem=part_send.at[p, k],
            recv_sem=part_recv.at[p, k], device_id={"col": lax.rem(col + k, cols)}, device_id_type=MESH)

    up_copy(0).start()
    up_copy(1).start()
    down_copy(0).start()
    down_copy(1).start()
    for p in range(passes):
        keep(p).start()
    pl.semaphore_wait(barrier, cols + 2)
    for p in range(passes):
        for k in range(1, cols):
            to_col(p, k).start()

    lane = lax.broadcasted_iota(jnp.int32, (BLOCK, lanes), 1)

    def move(p):
        for k in (1, 2, 3, 0):
            target = (row, partner, across, sibling)[k]

            def one(v, carry):
                first = target * (units * passes) + v
                result = gather[p][place_ref[first]]
                if passes == 2:
                    second = first + units
                    a = result.astype(jnp.float32)
                    b = gather[p][place_ref[second]].astype(jnp.float32)
                    a = jnp.where(lane_ref[first] == 0, a, pltpu.roll(a, piece, 1))
                    b = jnp.where(lane_ref[second] == 1, b, pltpu.roll(b, piece, 1))
                    result = jnp.where(lane < piece, a, b).astype(jnp.bfloat16)
                if k == 0:
                    blocks[p, 0, v] = result
                else:
                    moved[p, k - 1, v] = result
                return carry

            lax.fori_loop(0, units, one, 0, unroll=4)
            if k > 0:
                to_row(p, k).start()

    def lay(p):
        for k in range(4):
            origin = (row, partner, across, sibling)[k]
            at = (half if k >= 2 else 0) + lax.div(origin, 2) * piece

            def one(j, carry):
                tile = blocks[p, k, pl.ds(4 * j, 4)].reshape(4 * BLOCK, lanes).T
                for q in range(passes):
                    chunk = pl.ds(pl.multiple_of(q * units * BLOCK + 4 * BLOCK * j, 128), 4 * BLOCK)
                    panel[p, pl.ds(pl.multiple_of(at, piece), piece), chunk] = tile[q * piece:(q + 1) * piece]
                return carry

            lax.fori_loop(0, units // 4, one, 0)

    for p in range(passes):
        keep(p).wait()
        for k in range(1, cols):
            to_col(p, k).wait_recv()
        move(p)
    for k in (1, 2, 3):
        to_row(0, k).wait_recv()
    lay(0)

    def step(t, carry):
        for p in range(1, passes):
            @pl.when(t == p * chunks)
            def _():
                for k in (1, 2, 3):
                    to_row(p, k).wait_recv()
                lay(p)

        @pl.when(t < items)
        def _():
            up_copy(t).wait()
            slot = lax.rem(t, 2)

            @pl.when(t >= NEAR)
            def _():
                to_near(t - NEAR).wait_send()

            product = jnp.dot(panel[lax.div(t, chunks)], up_buf[slot], preferred_element_type=jnp.float32)
            near[lax.rem(t, NEAR)] = product[half:].astype(jnp.bfloat16)
            to_near(t).start()
            mine[slot] = product[:half]

            @pl.when(t + 2 < items)
            def _():
                up_copy(t + 2).start()

        @pl.when((t >= 1) & (t < items + 1))
        def _():
            item = t - 1
            to_near(item).wait_recv()
            far[item] = (mine[lax.rem(item, 2)] + hand[item].astype(jnp.float32)).astype(jnp.bfloat16)
            to_far(item).start()

        @pl.when((t >= LAG) & (t < items + LAG))
        def _():
            item = t - LAG
            to_far(item).wait_recv()
            summed = far[item].astype(jnp.float32) + hid[item, 0].astype(jnp.float32)
            hid[item, 0] = jnp.square(jnp.maximum(summed, 0.0)).astype(jnp.bfloat16)
            to_hid(item).start()

        @pl.when(t >= LAG + 1)
        def _():
            item = t - LAG - 1
            slot = lax.rem(item, 2)
            place = lax.rem(item, chunks)
            to_hid(item).wait_recv()
            down_copy(item).wait()
            hidden = hid[item].reshape(2 * half, width)
            tile = columns // 3
            for n in range(3):
                at = slice(n * tile, (n + 1) * tile)
                product = jnp.dot(hidden, down_buf[slot, :, at], preferred_element_type=jnp.float32)
                total[:, at] = jnp.where(place == 0, product, total[:, at] + product)

            @pl.when(item + 2 < items)
            def _():
                down_copy(item + 2).start()

            @pl.when(place == chunks - 1)
            def _():
                p = lax.div(item, chunks)
                for k in (*range(1, cols), 0):
                    target = lax.rem(col + k, cols)
                    origin = lax.div(target, piece // seg)
                    at = (lax.rem(origin + core, 2) * half + lax.div(origin, 2) * piece
                          + lax.rem(target, piece // seg) * seg)
                    own[p, k] = total[pl.ds(pl.multiple_of(at, seg), seg), :].astype(jnp.bfloat16)
                    if k > 0:
                        to_part(p, k).start()

        return carry

    lax.fori_loop(0, items + LAG + 1, step, 0)

    def drain(item, carry):
        to_far(item).wait_send()
        to_hid(item).wait_send()
        return carry

    lax.fori_loop(0, items, drain, 0)
    for item in range(max(items - NEAR, 0), items):
        to_near(item).wait_send()
    for p in range(passes):
        for k in range(1, cols):
            to_col(p, k).wait_send()
        for k in (1, 2, 3):
            to_row(p, k).wait_send()
    for p in range(passes):
        mixed = own[p, 0].astype(jnp.float32)
        for k in range(1, cols):
            to_part(p, k).wait_recv()
            mixed = mixed + parts[p, k].astype(jnp.float32)
        out_ref[p * seg:(p + 1) * seg, :] = mixed.astype(jnp.bfloat16)
    for p in range(passes):
        for k in range(1, cols):
            to_part(p, k).wait_send()


def layer(cols, place, lane, packed, up_weight, down_weight):
    passes, local_units, _, lanes = packed.shape
    depth, hidden = up_weight.shape
    columns = down_weight.shape[1]
    tokens = 4 * lanes // passes
    units = depth // BLOCK // passes
    width = next(w for w in (512, 384, 256, 128) if hidden % w == 0)
    chunks = hidden // width
    items = passes * chunks
    half = tokens // 2
    seg = tokens // cols
    flops = 2 * passes * tokens * hidden * (depth + columns)
    vmem = pl.BlockSpec(memory_space=pltpu.VMEM)
    smem = pl.BlockSpec(memory_space=pltpu.SMEM)
    hbm = pl.BlockSpec(memory_space=pl.ANY)
    dma = pltpu.SemaphoreType.DMA
    return pl.pallas_call(
        functools.partial(layer_kernel, passes, chunks, width),
        out_shape=jax.ShapeDtypeStruct((passes * seg, columns), jnp.bfloat16),
        in_specs=[smem, smem, vmem, hbm, hbm],
        out_specs=vmem,
        scratch_shapes=[pltpu.VMEM((cols * local_units, BLOCK, lanes), jnp.bfloat16)] * passes + [
            pltpu.VMEM((passes, 3, units, BLOCK, lanes), jnp.bfloat16),
            pltpu.VMEM((passes, 4, units, BLOCK, lanes), jnp.bfloat16),
            pltpu.VMEM((passes, tokens, depth), jnp.bfloat16),
            pltpu.VMEM((NEAR, half, width), jnp.bfloat16),
            pltpu.VMEM((2, half, width), jnp.float32),
            pltpu.VMEM((items, half, width), jnp.bfloat16),
            pltpu.VMEM((items, half, width), jnp.bfloat16),
            pltpu.VMEM((items, 2, half, width), jnp.bfloat16),
            pltpu.VMEM((tokens, columns), jnp.float32),
            pltpu.VMEM((passes, cols, seg, columns), jnp.bfloat16),
            pltpu.VMEM((passes, cols, seg, columns), jnp.bfloat16),
            pltpu.VMEM((2, depth, width), jnp.bfloat16),
            pltpu.VMEM((2, width, columns), jnp.bfloat16),
            dma((passes,)), dma((passes, cols)), dma((passes, cols)), dma((passes, 3)), dma((passes, 3)),
            dma((2,)), dma((2,)), dma((NEAR,)), dma((items,)), dma((items,)), dma((items,)),
            dma((items,)), dma((items,)), dma((passes, cols)), dma((passes, cols)),
        ],
        compiler_params=pltpu.CompilerParams(
            collective_id=0, has_side_effects=True, vmem_limit_bytes=60 * 1024 * 1024),
        cost_estimate=pl.CostEstimate(flops=flops, transcendentals=0,
                                      bytes_accessed=2 * passes * (up_weight.size + down_weight.size)),
    )(place, lane, packed, up_weight, down_weight)


def on_device(x_stored, group_units, group_order, up_weight, down_weight):
    rows, cols = lax.axis_size("row"), lax.axis_size("col")
    share, features = x_stored.shape
    passes = 2 if rows == cols else 1
    units = features // BLOCK // passes
    piece = share // passes
    packed = x_stored.reshape(passes, piece, passes, units, BLOCK).transpose(0, 3, 4, 2, 1)
    packed = block_scaled(packed.reshape(passes * units * BLOCK, share)).reshape(passes, units, BLOCK, share)
    source = unit_source(group_units, group_order)
    origin, inside = source // (units * passes), source % (units * passes)
    return layer(cols, origin * units + inside % units, inside // units, packed, up_weight, down_weight)


def solution(mesh):
    in_specs = (P(("groups", "row"), "col"), P(), P(), P("row", "col"), P("col", "row"))
    out_specs = P(("groups", "col"), "row")
    return jax.shard_map(
        on_device, mesh=mesh, in_specs=in_specs, out_specs=out_specs, check_vma=False
    )
```

```python
import functools
import jax
import jax.numpy as jnp
from jax import lax
from jax.experimental import pallas as pl
from jax.experimental.pallas import tpu as pltpu
from jax.sharding import PartitionSpec as P

BLOCK = 32
UNITS = 288
MESH = pl.DeviceIdType.MESH
LAG = 5
NEAR = 4


def unit_source(group_units, group_order):
    count = group_units.shape[0]
    group_ids = jnp.arange(count, dtype=jnp.int32)
    onehot = (group_order[:, None] == group_ids[None, :]).astype(jnp.int32)
    canon_start = jnp.cumsum(group_units) - group_units
    slot_length = jnp.sum(onehot * group_units[None, :], axis=1)
    slot_canon = jnp.sum(onehot * canon_start[None, :], axis=1)
    slot_start = jnp.cumsum(slot_length) - slot_length
    unit_ids = jnp.arange(UNITS, dtype=jnp.int32)
    inside = (unit_ids[:, None] >= slot_start[None, :]) & (
        unit_ids[:, None] < (slot_start + slot_length)[None, :]
    )
    canon_unit = jnp.sum(
        jnp.where(inside, slot_canon[None, :] + unit_ids[:, None] - slot_start[None, :], 0), axis=1
    )
    source = jnp.sum(
        jnp.where(canon_unit[None, :] == unit_ids[:, None], unit_ids[None, :], 0), axis=1
    )
    return source


def exponent_floor(magnitude, lowest, highest, offset):
    result = jnp.full(magnitude.shape, 2.0 ** (lowest + offset), jnp.float32)
    for power in range(lowest + 1, highest + 1):
        result = jnp.where(magnitude >= 2.0**power, jnp.float32(2.0 ** (power + offset)), result)
    return result


def block_scaled(values):
    features, tokens = values.shape
    blocks = values.astype(jnp.float32).reshape(features // BLOCK, BLOCK, tokens)
    largest = jnp.max(jnp.abs(blocks), axis=1)
    scale = exponent_floor(largest, -20, 8, -8)[:, None, :]
    magnitude = jnp.abs(blocks) / scale
    spacing = exponent_floor(magnitude, -6, 8, -3)
    level = jnp.minimum(jnp.floor(magnitude / spacing + 0.5) * spacing, 448.0)
    panels = jnp.where(blocks < 0.0, -level, level) * scale
    return panels.astype(jnp.bfloat16)


def tile_scaled(values):
    blocks = values.reshape(-1, BLOCK, values.shape[1])
    size = jnp.abs(blocks)
    largest = jnp.max(size, axis=1, keepdims=True)
    scale = jnp.full(largest.shape, 2.0**-28, jnp.float32)
    inverse = jnp.full(largest.shape, 2.0**28, jnp.float32)
    for power in range(-19, 9):
        above = largest >= 2.0**power
        scale = jnp.where(above, jnp.float32(2.0 ** (power - 8)), scale)
        inverse = jnp.where(above, jnp.float32(2.0 ** (8 - power)), inverse)
    size = size * inverse
    nudged = size * (1.0 + 2.0**-12)
    wide = nudged * (2.0**20 + 1.0)
    level = jnp.where(size < 2.0**-6, jnp.floor(size * 512.0 + 0.5) * (1.0 / 512.0), wide - (wide - nudged))
    level = jnp.minimum(level, 448.0) * scale
    return jnp.where(blocks < 0.0, -level, level)


def layer_kernel(passes, chunks, width, *refs):
    place_ref, lane_ref, raw_ref, up_ref, down_ref, out_ref = refs[:6]
    gather = refs[6:6 + passes]
    (x_ref, moved, blocks, panel, near, mine, hand, far, hid, total, own, parts, up_buf, down_buf,
     keep_sem, gather_send, gather_recv, moved_send, moved_recv, relay_send, relay_recv, up_sem, down_sem, near_send, near_recv,
     far_send, far_recv, hid_send, hid_recv, part_send, part_recv) = refs[6 + passes:]
    items = passes * chunks
    half = hand.shape[1]
    cols, seg = own.shape[1], own.shape[2]
    units, lanes = blocks.shape[2], blocks.shape[4]
    local = x_ref.shape[1]
    piece = lanes // passes
    columns = out_ref.shape[1]
    row, col = lax.axis_index("row"), lax.axis_index("col")
    core = lax.rem(row, 2)
    relay = units % cols == 0
    count = units // cols if relay else units
    first_unit = col * count if relay else 0
    part = pl.ds(first_unit, count)
    sibling = row + 1 - 2 * core
    partner = lax.rem(row + 2, 4)
    across = lax.rem(sibling + 2, 4)

    barrier = pltpu.get_barrier_semaphore()
    for other in (sibling, partner, across):
        pl.semaphore_signal(barrier, inc=1, device_id={"row": other}, device_id_type=MESH)
    for k in range(1, cols):
        pl.semaphore_signal(barrier, inc=1, device_id={"col": lax.rem(col + k, cols)}, device_id_type=MESH)

    def keep(p):
        return pltpu.make_async_copy(x_ref.at[p], gather[p].at[pl.ds(col * local, local)], keep_sem.at[p])

    def to_col(p, k):
        return pltpu.make_async_remote_copy(
            src_ref=x_ref.at[p], dst_ref=gather[p].at[pl.ds(col * local, local)], send_sem=gather_send.at[p, k],
            recv_sem=gather_recv.at[p, k], device_id={"col": lax.rem(col + k, cols)}, device_id_type=MESH)

    def to_row(p, k):
        target = (row, partner, across, sibling)[k]
        mine_of = slice(None) if k == 3 else part
        return pltpu.make_async_remote_copy(
            src_ref=moved.at[p, k - 1, mine_of], dst_ref=blocks.at[p, k, mine_of], send_sem=moved_send.at[p, k - 1],
            recv_sem=moved_recv.at[p, k - 1], device_id={"row": target}, device_id_type=MESH)

    def to_relay(p, k, m):
        return pltpu.make_async_remote_copy(
            src_ref=blocks.at[p, k, part], dst_ref=blocks.at[p, k, part], send_sem=relay_send.at[p, k - 1, m],
            recv_sem=relay_recv.at[p, k - 1, m], device_id={"col": lax.rem(col + m, cols)}, device_id_type=MESH)

    def up_copy(item):
        slot = lax.rem(item, 2)
        chunk = pl.ds(pl.multiple_of(lax.rem(item, chunks) * width, width), width)
        return pltpu.make_async_copy(up_ref.at[:, chunk], up_buf.at[slot], up_sem.at[slot])

    def down_copy(item):
        slot = lax.rem(item, 2)
        chunk = pl.ds(pl.multiple_of(lax.rem(item, chunks) * width, width), width)
        return pltpu.make_async_copy(down_ref.at[chunk, :], down_buf.at[slot], down_sem.at[slot])

    def to_near(item):
        slot = lax.rem(item, NEAR)
        return pltpu.make_async_remote_copy(
            src_ref=near.at[slot], dst_ref=hand.at[item], send_sem=near_send.at[slot],
            recv_sem=near_recv.at[item], device_id={"row": sibling}, device_id_type=MESH)

    def to_far(item):
        return pltpu.make_async_remote_copy(
            src_ref=far.at[item], dst_ref=hid.at[item, 0], send_sem=far_send.at[item],
            recv_sem=far_recv.at[item], device_id={"row": partner}, device_id_type=MESH)

    def to_hid(item):
        return pltpu.make_async_remote_copy(
            src_ref=hid.at[item, 0], dst_ref=hid.at[item, 1], send_sem=hid_send.at[item],
            recv_sem=hid_recv.at[item], device_id={"row": sibling}, device_id_type=MESH)

    def to_part(p, k):
        return pltpu.make_async_remote_copy(
            src_ref=own.at[p, k], dst_ref=parts.at[p, k], send_sem=part_send.at[p, k],
            recv_sem=part_recv.at[p, k], device_id={"col": lax.rem(col + k, cols)}, device_id_type=MESH)

    up_copy(0).start()
    up_copy(1).start()
    down_copy(0).start()
    down_copy(1).start()

    if raw_ref.ndim == 4:
        x_ref[...] = raw_ref[...]
    else:
        wide_lane = lax.broadcasted_iota(jnp.int32, (4 * BLOCK, lanes), 1)

        def encode(j, carry):
            def tile(q):
                chunk = pl.ds(pl.multiple_of(q * units * BLOCK + 4 * BLOCK * j, 128), 4 * BLOCK)
                return tile_scaled(raw_ref[:, chunk].astype(jnp.float32).T).reshape(4 * BLOCK, lanes)

            if passes == 1:
                packed = [tile(0)]
            else:
                a, b = tile(0), tile(1)
                packed = [jnp.where(wide_lane < piece, a, pltpu.roll(b, piece, 1)),
                          jnp.where(wide_lane < piece, pltpu.roll(a, piece, 1), b)]
            for p in range(passes):
                x_ref[p, pl.ds(4 * j, 4)] = packed[p].astype(jnp.bfloat16).reshape(4, BLOCK, lanes)
            return carry

        lax.fori_loop(0, local // 4, encode, 0)

    for p in range(passes):
        keep(p).start()
    pl.semaphore_wait(barrier, cols + 2)
    for k in range(1, cols):
        to_col(0, k).start()

    lane = lax.broadcasted_iota(jnp.int32, (BLOCK, lanes), 1)

    def move(p):
        for k in (1, 2, 3, 0):
            target = (row, partner, across, sibling)[k]

            begin, length = (first_unit, count) if k in (1, 2) else (0, units)

            def one(step_of, carry):
                v = begin + step_of
                first = target * (units * passes) + v
                result = gather[p][place_ref[first]]
                if passes == 2:
                    second = first + units
                    a = result.astype(jnp.float32)
                    b = gather[p][place_ref[second]].astype(jnp.float32)
                    a = jnp.where(lane_ref[first] == 0, a, pltpu.roll(a, piece, 1))
                    b = jnp.where(lane_ref[second] == 1, b, pltpu.roll(b, piece, 1))
                    result = jnp.where(lane < piece, a, b).astype(jnp.bfloat16)
                if k == 0:
                    blocks[p, 0, v] = result
                else:
                    moved[p, k - 1, v] = result
                return carry

            lax.fori_loop(0, length, one, 0, unroll=4 if length % 4 == 0 else 3)
            if k > 0:
                to_row(p, k).start()

    def lay(p):
        for k in range(4):
            origin = (row, partner, across, sibling)[k]
            at = (half if k >= 2 else 0) + lax.div(origin, 2) * piece

            def one(j, carry):
                tile = blocks[p, k, pl.ds(4 * j, 4)].reshape(4 * BLOCK, lanes).T
                for q in range(passes):
                    chunk = pl.ds(pl.multiple_of(q * units * BLOCK + 4 * BLOCK * j, 128), 4 * BLOCK)
                    panel[p, pl.ds(pl.multiple_of(at, piece), piece), chunk] = tile[q * piece:(q + 1) * piece]
                return carry

            lax.fori_loop(0, units // 4, one, 0)

    def collect(p):
        keep(p).wait()
        for k in range(1, cols):
            to_col(p, k).wait_recv()
        move(p)

    def hand_on(p):
        for k in (1, 2):
            to_row(p, k).wait_recv()
            if relay:
                for m in range(1, cols):
                    to_relay(p, k, m).start()

    def finish(p):
        to_row(p, 3).wait_recv()
        if relay:
            for k in (1, 2):
                for m in range(1, cols):
                    to_relay(p, k, m).wait_recv()
        lay(p)

    collect(0)
    hand_on(0)
    for p in range(1, passes):
        for k in range(1, cols):
            to_col(p, k).start()
    finish(0)

    def step(t, carry):
        for p in range(1, passes):
            begin = (p - 1) * chunks + chunks // 2
            pl.when(t == begin)(functools.partial(collect, p))
            pl.when(t == begin + 3)(functools.partial(hand_on, p))
            pl.when(t == p * chunks)(functools.partial(finish, p))

        @pl.when(t < items)
        def _():
            up_copy(t).wait()
            slot = lax.rem(t, 2)

            @pl.when(t >= NEAR)
            def _():
                to_near(t - NEAR).wait_send()

            product = jnp.dot(panel[lax.div(t, chunks)], up_buf[slot], preferred_element_type=jnp.float32)
            near[lax.rem(t, NEAR)] = product[half:].astype(jnp.bfloat16)
            to_near(t).start()
            mine[slot] = product[:half]

            @pl.when(t + 2 < items)
            def _():
                up_copy(t + 2).start()

        @pl.when((t >= 1) & (t < items + 1))
        def _():
            item = t - 1
            to_near(item).wait_recv()
            far[item] = (mine[lax.rem(item, 2)] + hand[item].astype(jnp.float32)).astype(jnp.bfloat16)
            to_far(item).start()

        @pl.when((t >= LAG) & (t < items + LAG))
        def _():
            item = t - LAG
            to_far(item).wait_recv()
            summed = far[item].astype(jnp.float32) + hid[item, 0].astype(jnp.float32)
            hid[item, 0] = jnp.square(jnp.maximum(summed, 0.0)).astype(jnp.bfloat16)
            to_hid(item).start()

        @pl.when(t >= LAG + 1)
        def _():
            item = t - LAG - 1
            slot = lax.rem(item, 2)
            place = lax.rem(item, chunks)
            to_hid(item).wait_recv()
            down_copy(item).wait()
            hidden = hid[item].reshape(2 * half, width)
            tile = columns // 3
            for n in range(3):
                at = slice(n * tile, (n + 1) * tile)
                product = jnp.dot(hidden, down_buf[slot, :, at], preferred_element_type=jnp.float32)
                total[:, at] = jnp.where(place == 0, product, total[:, at] + product)

            @pl.when(item + 2 < items)
            def _():
                down_copy(item + 2).start()

            @pl.when(place == chunks - 1)
            def _():
                p = lax.div(item, chunks)
                for k in (*range(1, cols), 0):
                    target = lax.rem(col + k, cols)
                    origin = lax.div(target, piece // seg)
                    at = (lax.rem(origin + core, 2) * half + lax.div(origin, 2) * piece
                          + lax.rem(target, piece // seg) * seg)
                    own[p, k] = total[pl.ds(pl.multiple_of(at, seg), seg), :].astype(jnp.bfloat16)
                    if k > 0:
                        to_part(p, k).start()

        return carry

    lax.fori_loop(0, items + LAG + 1, step, 0)

    def drain(item, carry):
        to_far(item).wait_send()
        to_hid(item).wait_send()
        return carry

    lax.fori_loop(0, items, drain, 0)
    for item in range(max(items - NEAR, 0), items):
        to_near(item).wait_send()
    for p in range(passes):
        for k in range(1, cols):
            to_col(p, k).wait_send()
        for k in (1, 2, 3):
            to_row(p, k).wait_send()
        if relay:
            for k in (1, 2):
                for m in range(1, cols):
                    to_relay(p, k, m).wait_send()
    for p in range(passes):
        mixed = own[p, 0].astype(jnp.float32)
        for k in range(1, cols):
            to_part(p, k).wait_recv()
            mixed = mixed + parts[p, k].astype(jnp.float32)
        out_ref[p * seg:(p + 1) * seg, :] = mixed.astype(jnp.bfloat16)
    for p in range(passes):
        for k in range(1, cols):
            to_part(p, k).wait_send()


def layer(cols, passes, place, lane, values, up_weight, down_weight):
    if values.ndim == 4:
        local_units, lanes = values.shape[1], values.shape[3]
    else:
        local_units, lanes = values.shape[1] // BLOCK // passes, values.shape[0]
    depth, hidden = up_weight.shape
    columns = down_weight.shape[1]
    tokens = 4 * lanes // passes
    units = depth // BLOCK // passes
    width = next(w for w in (512, 384, 256, 128) if hidden % w == 0)
    chunks = hidden // width
    items = passes * chunks
    half = tokens // 2
    seg = tokens // cols
    flops = 2 * passes * tokens * hidden * (depth + columns)
    vmem = pl.BlockSpec(memory_space=pltpu.VMEM)
    smem = pl.BlockSpec(memory_space=pltpu.SMEM)
    hbm = pl.BlockSpec(memory_space=pl.ANY)
    dma = pltpu.SemaphoreType.DMA
    return pl.pallas_call(
        functools.partial(layer_kernel, passes, chunks, width),
        out_shape=jax.ShapeDtypeStruct((passes * seg, columns), jnp.bfloat16),
        in_specs=[smem, smem, vmem, hbm, hbm],
        out_specs=vmem,
        scratch_shapes=[pltpu.VMEM((cols * local_units, BLOCK, lanes), jnp.bfloat16)] * passes + [
            pltpu.VMEM((passes, local_units, BLOCK, lanes), jnp.bfloat16),
            pltpu.VMEM((passes, 3, units, BLOCK, lanes), jnp.bfloat16),
            pltpu.VMEM((passes, 4, units, BLOCK, lanes), jnp.bfloat16),
            pltpu.VMEM((passes, tokens, depth), jnp.bfloat16),
            pltpu.VMEM((NEAR, half, width), jnp.bfloat16),
            pltpu.VMEM((2, half, width), jnp.float32),
            pltpu.VMEM((items, half, width), jnp.bfloat16),
            pltpu.VMEM((items, half, width), jnp.bfloat16),
            pltpu.VMEM((items, 2, half, width), jnp.bfloat16),
            pltpu.VMEM((tokens, columns), jnp.float32),
            pltpu.VMEM((passes, cols, seg, columns), jnp.bfloat16),
            pltpu.VMEM((passes, cols, seg, columns), jnp.bfloat16),
            pltpu.VMEM((2, depth, width), jnp.bfloat16),
            pltpu.VMEM((2, width, columns), jnp.bfloat16),
            dma((passes,)), dma((passes, cols)), dma((passes, cols)), dma((passes, 3)), dma((passes, 3)),
            dma((passes, 2, cols)), dma((passes, 2, cols)),
            dma((2,)), dma((2,)), dma((NEAR,)), dma((items,)), dma((items,)), dma((items,)),
            dma((items,)), dma((items,)), dma((passes, cols)), dma((passes, cols)),
        ],
        compiler_params=pltpu.CompilerParams(
            collective_id=0, has_side_effects=True, vmem_limit_bytes=60 * 1024 * 1024),
        cost_estimate=pl.CostEstimate(flops=flops, transcendentals=0,
                                      bytes_accessed=2 * passes * (up_weight.size + down_weight.size)),
    )(place, lane, values, up_weight, down_weight)


def on_device(x_stored, group_units, group_order, up_weight, down_weight):
    rows, cols = lax.axis_size("row"), lax.axis_size("col")
    share, features = x_stored.shape
    passes = 2 if rows == cols else 1
    units = features // BLOCK // passes
    piece = share // passes
    values = x_stored
    if features % (128 * passes) != 0:
        packed = x_stored.reshape(passes, piece, passes, units, BLOCK).transpose(0, 3, 4, 2, 1)
        packed = block_scaled(packed.reshape(passes * units * BLOCK, share))
        values = packed.reshape(passes, units, BLOCK, share)
    source = unit_source(group_units, group_order)
    origin, inside = source // (units * passes), source % (units * passes)
    return layer(cols, passes, origin * units + inside % units, inside // units, values, up_weight, down_weight)


def solution(mesh):
    in_specs = (P(("groups", "row"), "col"), P(), P(), P("row", "col"), P("col", "row"))
    out_specs = P(("groups", "col"), "row")
    return jax.shard_map(
        on_device, mesh=mesh, in_specs=in_specs, out_specs=out_specs, check_vma=False
    )
```

```python
import functools
import jax
import jax.numpy as jnp
from jax import lax
from jax.experimental import pallas as pl
from jax.experimental.pallas import tpu as pltpu
from jax.sharding import PartitionSpec as P

BLOCK = 32
UNITS = 288
MESH = pl.DeviceIdType.MESH
LAG = 8
NEAR = 4


def unit_source(group_units, group_order):
    count = group_units.shape[0]
    group_ids = jnp.arange(count, dtype=jnp.int32)
    onehot = (group_order[:, None] == group_ids[None, :]).astype(jnp.int32)
    canon_start = jnp.cumsum(group_units) - group_units
    slot_length = jnp.sum(onehot * group_units[None, :], axis=1)
    slot_canon = jnp.sum(onehot * canon_start[None, :], axis=1)
    slot_start = jnp.cumsum(slot_length) - slot_length
    unit_ids = jnp.arange(UNITS, dtype=jnp.int32)
    inside = (unit_ids[:, None] >= slot_start[None, :]) & (
        unit_ids[:, None] < (slot_start + slot_length)[None, :]
    )
    canon_unit = jnp.sum(
        jnp.where(inside, slot_canon[None, :] + unit_ids[:, None] - slot_start[None, :], 0), axis=1
    )
    source = jnp.sum(
        jnp.where(canon_unit[None, :] == unit_ids[:, None], unit_ids[None, :], 0), axis=1
    )
    return source


def exponent_floor(magnitude, lowest, highest, offset):
    result = jnp.full(magnitude.shape, 2.0 ** (lowest + offset), jnp.float32)
    for power in range(lowest + 1, highest + 1):
        result = jnp.where(magnitude >= 2.0**power, jnp.float32(2.0 ** (power + offset)), result)
    return result


def block_scaled(values):
    features, tokens = values.shape
    blocks = values.astype(jnp.float32).reshape(features // BLOCK, BLOCK, tokens)
    largest = jnp.max(jnp.abs(blocks), axis=1)
    scale = exponent_floor(largest, -20, 8, -8)[:, None, :]
    magnitude = jnp.abs(blocks) / scale
    spacing = exponent_floor(magnitude, -6, 8, -3)
    level = jnp.minimum(jnp.floor(magnitude / spacing + 0.5) * spacing, 448.0)
    panels = jnp.where(blocks < 0.0, -level, level) * scale
    return panels.astype(jnp.bfloat16)


def tile_scaled(values):
    blocks = values.reshape(-1, BLOCK, values.shape[1])
    size = jnp.abs(blocks)
    largest = jnp.max(size, axis=1, keepdims=True)
    scale = jnp.full(largest.shape, 2.0**-28, jnp.float32)
    inverse = jnp.full(largest.shape, 2.0**28, jnp.float32)
    for power in range(-19, 9):
        above = largest >= 2.0**power
        scale = jnp.where(above, jnp.float32(2.0 ** (power - 8)), scale)
        inverse = jnp.where(above, jnp.float32(2.0 ** (8 - power)), inverse)
    size = size * inverse
    nudged = size * (1.0 + 2.0**-12)
    wide = nudged * (2.0**20 + 1.0)
    level = jnp.where(size < 2.0**-6, jnp.floor(size * 512.0 + 0.5) * (1.0 / 512.0), wide - (wide - nudged))
    level = jnp.minimum(level, 448.0) * scale
    return jnp.where(blocks < 0.0, -level, level)


def layer_kernel(passes, turns, chunks, width, *refs):
    place_ref, lane_ref, raw_ref, up_ref, down_ref, out_ref = refs[:6]
    gather = refs[6:6 + passes]
    (x_ref, moved, blocks, panel, near, mine, hand, far, hid, total, own, parts, up_buf, down_buf,
     keep_sem, gather_send, gather_recv, moved_send, moved_recv, relay_send, relay_recv, up_sem, down_sem, near_send, near_recv,
     far_send, far_recv, hid_send, hid_recv, part_send, part_recv) = refs[6 + passes:]
    items = turns * chunks
    split = turns // passes
    half = hand.shape[1]
    cols, seg = own.shape[1], own.shape[2]
    units, lanes = blocks.shape[2], blocks.shape[4]
    local = x_ref.shape[1]
    piece = lanes // passes
    small = piece // split
    columns = out_ref.shape[1]
    row, col = lax.axis_index("row"), lax.axis_index("col")
    core = lax.rem(row, 2)
    relay = units % cols == 0
    count = units // cols if relay else units
    first_unit = col * count if relay else 0
    part = pl.ds(first_unit, count)
    sibling = row + 1 - 2 * core
    partner = lax.rem(row + 2, 4)
    across = lax.rem(sibling + 2, 4)

    barrier = pltpu.get_barrier_semaphore()
    for other in (sibling, partner, across):
        pl.semaphore_signal(barrier, inc=1, device_id={"row": other}, device_id_type=MESH)
    for k in range(1, cols):
        pl.semaphore_signal(barrier, inc=1, device_id={"col": lax.rem(col + k, cols)}, device_id_type=MESH)

    def keep(p):
        return pltpu.make_async_copy(x_ref.at[p], gather[p].at[pl.ds(col * local, local)], keep_sem.at[p])

    def to_col(p, k):
        return pltpu.make_async_remote_copy(
            src_ref=x_ref.at[p], dst_ref=gather[p].at[pl.ds(col * local, local)], send_sem=gather_send.at[p, k],
            recv_sem=gather_recv.at[p, k], device_id={"col": lax.rem(col + k, cols)}, device_id_type=MESH)

    def to_row(p, k):
        target = (row, partner, across, sibling)[k]
        mine_of = slice(None) if k == 3 else part
        return pltpu.make_async_remote_copy(
            src_ref=moved.at[p, k - 1, mine_of], dst_ref=blocks.at[p, k, mine_of], send_sem=moved_send.at[p, k - 1],
            recv_sem=moved_recv.at[p, k - 1], device_id={"row": target}, device_id_type=MESH)

    def to_relay(p, k, m):
        return pltpu.make_async_remote_copy(
            src_ref=blocks.at[p, k, part], dst_ref=blocks.at[p, k, part], send_sem=relay_send.at[p, k - 1, m],
            recv_sem=relay_recv.at[p, k - 1, m], device_id={"col": lax.rem(col + m, cols)}, device_id_type=MESH)

    def up_copy(item):
        slot = lax.rem(item, 2)
        chunk = pl.ds(pl.multiple_of(lax.rem(item, chunks) * width, width), width)
        return pltpu.make_async_copy(up_ref.at[:, chunk], up_buf.at[slot], up_sem.at[slot])

    def down_copy(item):
        slot = lax.rem(item, 2)
        chunk = pl.ds(pl.multiple_of(lax.rem(item, chunks) * width, width), width)
        return pltpu.make_async_copy(down_ref.at[chunk, :], down_buf.at[slot], down_sem.at[slot])

    def to_near(item):
        slot = lax.rem(item, NEAR)
        return pltpu.make_async_remote_copy(
            src_ref=near.at[slot], dst_ref=hand.at[item], send_sem=near_send.at[slot],
            recv_sem=near_recv.at[item], device_id={"row": sibling}, device_id_type=MESH)

    def to_far(item):
        return pltpu.make_async_remote_copy(
            src_ref=far.at[item], dst_ref=hid.at[item, 0], send_sem=far_send.at[item],
            recv_sem=far_recv.at[item], device_id={"row": partner}, device_id_type=MESH)

    def to_hid(item):
        return pltpu.make_async_remote_copy(
            src_ref=hid.at[item, 0], dst_ref=hid.at[item, 1], send_sem=hid_send.at[item],
            recv_sem=hid_recv.at[item], device_id={"row": sibling}, device_id_type=MESH)

    def to_part(p, k):
        return pltpu.make_async_remote_copy(
            src_ref=own.at[p, k], dst_ref=parts.at[p, k], send_sem=part_send.at[p, k],
            recv_sem=part_recv.at[p, k], device_id={"col": lax.rem(col + k, cols)}, device_id_type=MESH)

    up_copy(0).start()
    up_copy(1).start()
    down_copy(0).start()
    down_copy(1).start()

    if raw_ref.ndim == 4:
        x_ref[...] = raw_ref[...]
    else:
        wide_lane = lax.broadcasted_iota(jnp.int32, (4 * BLOCK, lanes), 1)

        def encode(j, carry):
            def tile(q):
                chunk = pl.ds(pl.multiple_of(q * units * BLOCK + 4 * BLOCK * j, 128), 4 * BLOCK)
                return tile_scaled(raw_ref[:, chunk].astype(jnp.float32).T).reshape(4 * BLOCK, lanes)

            if passes == 1:
                packed = [tile(0)]
            else:
                a, b = tile(0), tile(1)
                packed = [jnp.where(wide_lane < piece, a, pltpu.roll(b, piece, 1)),
                          jnp.where(wide_lane < piece, pltpu.roll(a, piece, 1), b)]
            for p in range(passes):
                x_ref[p, pl.ds(4 * j, 4)] = packed[p].astype(jnp.bfloat16).reshape(4, BLOCK, lanes)
            return carry

        lax.fori_loop(0, local // 4, encode, 0)

    for p in range(passes):
        keep(p).start()
    pl.semaphore_wait(barrier, cols + 2)
    for k in range(1, cols):
        to_col(0, k).start()

    lane = lax.broadcasted_iota(jnp.int32, (BLOCK, lanes), 1)

    def move(p):
        for k in (1, 2, 3, 0):
            target = (row, partner, across, sibling)[k]

            begin, length = (first_unit, count) if k in (1, 2) else (0, units)

            def one(step_of, carry):
                v = begin + step_of
                first = target * (units * passes) + v
                result = gather[p][place_ref[first]]
                if passes == 2:
                    second = first + units
                    a = result.astype(jnp.float32)
                    b = gather[p][place_ref[second]].astype(jnp.float32)
                    a = jnp.where(lane_ref[first] == 0, a, pltpu.roll(a, piece, 1))
                    b = jnp.where(lane_ref[second] == 1, b, pltpu.roll(b, piece, 1))
                    result = jnp.where(lane < piece, a, b).astype(jnp.bfloat16)
                if k == 0:
                    blocks[p, 0, v] = result
                else:
                    moved[p, k - 1, v] = result
                return carry

            lax.fori_loop(0, length, one, 0, unroll=4 if length % 4 == 0 else 3)
            if k > 0:
                to_row(p, k).start()

    def lay(p):
        for k in range(4):
            origin = (row, partner, across, sibling)[k]
            at = (half if k >= 2 else 0) + lax.div(origin, 2) * small

            def one(j, carry):
                tile = blocks[p, k, pl.ds(4 * j, 4)].reshape(4 * BLOCK, lanes).T
                for q in range(passes):
                    chunk = pl.ds(pl.multiple_of(q * units * BLOCK + 4 * BLOCK * j, 128), 4 * BLOCK)
                    for i in range(split):
                        first = q * piece + i * small
                        panel[p * split + i, pl.ds(pl.multiple_of(at, small), small), chunk] = tile[first:first + small]
                return carry

            lax.fori_loop(0, units // 4, one, 0)

    def collect(p):
        keep(p).wait()
        for k in range(1, cols):
            to_col(p, k).wait_recv()
        move(p)

    def hand_on(p):
        for k in (1, 2):
            to_row(p, k).wait_recv()
            if relay:
                for m in range(1, cols):
                    to_relay(p, k, m).start()

    def finish(p):
        to_row(p, 3).wait_recv()
        if relay:
            for k in (1, 2):
                for m in range(1, cols):
                    to_relay(p, k, m).wait_recv()
        lay(p)

    collect(0)
    hand_on(0)
    for p in range(1, passes):
        for k in range(1, cols):
            to_col(p, k).start()
    finish(0)

    def step(t, carry):
        for p in range(1, passes):
            end = p * split * chunks
            pl.when(t == end - (split * chunks) // 2)(functools.partial(collect, p))
            pl.when(t == end - (split * chunks) // 3)(functools.partial(hand_on, p))
            pl.when(t == end)(functools.partial(finish, p))

        @pl.when(t < items)
        def _():
            up_copy(t).wait()
            slot = lax.rem(t, 2)

            @pl.when(t >= NEAR)
            def _():
                to_near(t - NEAR).wait_send()

            product = jnp.dot(panel[lax.div(t, chunks)], up_buf[slot], preferred_element_type=jnp.float32)
            near[lax.rem(t, NEAR)] = product[half:].astype(jnp.bfloat16)
            to_near(t).start()
            mine[slot] = product[:half]

            @pl.when(t + 2 < items)
            def _():
                up_copy(t + 2).start()

        @pl.when((t >= 1) & (t < items + 1))
        def _():
            item = t - 1
            to_near(item).wait_recv()
            far[item] = (mine[lax.rem(item, 2)] + hand[item].astype(jnp.float32)).astype(jnp.bfloat16)
            to_far(item).start()

        @pl.when((t >= LAG) & (t < items + LAG))
        def _():
            item = t - LAG
            to_far(item).wait_recv()
            summed = far[item].astype(jnp.float32) + hid[item, 0].astype(jnp.float32)
            hid[item, 0] = jnp.square(jnp.maximum(summed, 0.0)).astype(jnp.bfloat16)
            to_hid(item).start()

        @pl.when(t >= LAG + 1)
        def _():
            item = t - LAG - 1
            slot = lax.rem(item, 2)
            place = lax.rem(item, chunks)
            to_hid(item).wait_recv()
            down_copy(item).wait()
            hidden = hid[item].reshape(2 * half, width)
            tile = columns // 3
            for n in range(3):
                at = slice(n * tile, (n + 1) * tile)
                product = jnp.dot(hidden, down_buf[slot, :, at], preferred_element_type=jnp.float32)
                total[:, at] = jnp.where(place == 0, product, total[:, at] + product)

            @pl.when(item + 2 < items)
            def _():
                down_copy(item + 2).start()

            @pl.when(place == chunks - 1)
            def _():
                p = lax.div(item, chunks)
                for k in (*range(1, cols), 0):
                    target = lax.rem(col + k, cols)
                    origin = lax.div(target, small // seg)
                    at = (lax.rem(origin + core, 2) * half + lax.div(origin, 2) * small
                          + lax.rem(target, small // seg) * seg)
                    own[p, k] = total[pl.ds(pl.multiple_of(at, seg), seg), :].astype(jnp.bfloat16)
                    if k > 0:
                        to_part(p, k).start()

        return carry

    lax.fori_loop(0, items + LAG + 1, step, 0)

    def drain(item, carry):
        to_far(item).wait_send()
        to_hid(item).wait_send()
        return carry

    lax.fori_loop(0, items, drain, 0)
    for item in range(max(items - NEAR, 0), items):
        to_near(item).wait_send()
    for p in range(passes):
        for k in range(1, cols):
            to_col(p, k).wait_send()
        for k in (1, 2, 3):
            to_row(p, k).wait_send()
        if relay:
            for k in (1, 2):
                for m in range(1, cols):
                    to_relay(p, k, m).wait_send()
    for p in range(turns):
        mixed = own[p, 0].astype(jnp.float32)
        for k in range(1, cols):
            to_part(p, k).wait_recv()
            mixed = mixed + parts[p, k].astype(jnp.float32)
        out_ref[p * seg:(p + 1) * seg, :] = mixed.astype(jnp.bfloat16)
    for p in range(turns):
        for k in range(1, cols):
            to_part(p, k).wait_send()


def layer(cols, passes, place, lane, values, up_weight, down_weight):
    if values.ndim == 4:
        local_units, lanes = values.shape[1], values.shape[3]
    else:
        local_units, lanes = values.shape[1] // BLOCK // passes, values.shape[0]
    depth, hidden = up_weight.shape
    columns = down_weight.shape[1]
    turns = 2 * passes if (lanes // passes) % 32 == 0 and passes > 1 else passes
    tokens = 4 * lanes // turns
    units = depth // BLOCK // passes
    width = next(w for w in (512, 384, 256, 128) if hidden % w == 0)
    chunks = hidden // width
    items = turns * chunks
    half = tokens // 2
    seg = tokens // cols
    flops = 2 * turns * tokens * hidden * (depth + columns)
    vmem = pl.BlockSpec(memory_space=pltpu.VMEM)
    smem = pl.BlockSpec(memory_space=pltpu.SMEM)
    hbm = pl.BlockSpec(memory_space=pl.ANY)
    dma = pltpu.SemaphoreType.DMA
    return pl.pallas_call(
        functools.partial(layer_kernel, passes, turns, chunks, width),
        out_shape=jax.ShapeDtypeStruct((turns * seg, columns), jnp.bfloat16),
        in_specs=[smem, smem, vmem, hbm, hbm],
        out_specs=vmem,
        scratch_shapes=[pltpu.VMEM((cols * local_units, BLOCK, lanes), jnp.bfloat16)] * passes + [
            pltpu.VMEM((passes, local_units, BLOCK, lanes), jnp.bfloat16),
            pltpu.VMEM((passes, 3, units, BLOCK, lanes), jnp.bfloat16),
            pltpu.VMEM((passes, 4, units, BLOCK, lanes), jnp.bfloat16),
            pltpu.VMEM((turns, tokens, depth), jnp.bfloat16),
            pltpu.VMEM((NEAR, half, width), jnp.bfloat16),
            pltpu.VMEM((2, half, width), jnp.float32),
            pltpu.VMEM((items, half, width), jnp.bfloat16),
            pltpu.VMEM((items, half, width), jnp.bfloat16),
            pltpu.VMEM((items, 2, half, width), jnp.bfloat16),
            pltpu.VMEM((tokens, columns), jnp.float32),
            pltpu.VMEM((turns, cols, seg, columns), jnp.bfloat16),
            pltpu.VMEM((turns, cols, seg, columns), jnp.bfloat16),
            pltpu.VMEM((2, depth, width), jnp.bfloat16),
            pltpu.VMEM((2, width, columns), jnp.bfloat16),
            dma((passes,)), dma((passes, cols)), dma((passes, cols)), dma((passes, 3)), dma((passes, 3)),
            dma((passes, 2, cols)), dma((passes, 2, cols)),
            dma((2,)), dma((2,)), dma((NEAR,)), dma((items,)), dma((items,)), dma((items,)),
            dma((items,)), dma((items,)), dma((turns, cols)), dma((turns, cols)),
        ],
        compiler_params=pltpu.CompilerParams(
            collective_id=0, has_side_effects=True, vmem_limit_bytes=60 * 1024 * 1024),
        cost_estimate=pl.CostEstimate(flops=flops, transcendentals=0,
                                      bytes_accessed=2 * turns * (up_weight.size + down_weight.size)),
    )(place, lane, values, up_weight, down_weight)


def on_device(x_stored, group_units, group_order, up_weight, down_weight):
    rows, cols = lax.axis_size("row"), lax.axis_size("col")
    share, features = x_stored.shape
    passes = 2 if rows == cols else 1
    units = features // BLOCK // passes
    piece = share // passes
    values = x_stored
    if features % (128 * passes) != 0:
        packed = x_stored.reshape(passes, piece, passes, units, BLOCK).transpose(0, 3, 4, 2, 1)
        packed = block_scaled(packed.reshape(passes * units * BLOCK, share))
        values = packed.reshape(passes, units, BLOCK, share)
    source = unit_source(group_units, group_order)
    origin, inside = source // (units * passes), source % (units * passes)
    return layer(cols, passes, origin * units + inside % units, inside // units, values, up_weight, down_weight)


def solution(mesh):
    in_specs = (P(("groups", "row"), "col"), P(), P(), P("row", "col"), P("col", "row"))
    out_specs = P(("groups", "col"), "row")
    return jax.shard_map(
        on_device, mesh=mesh, in_specs=in_specs, out_specs=out_specs, check_vma=False
    )
```
